32 devices in a mesh: region: 4 (over y, core), node: 8 (over z, x).
Axes of the slice: x: 2, y: 2, z: 4, core: 2. Of those that a mesh axis runs over, the one named last changes fastest.
Arguments:
- impedance: float32 [8, 4096, 4096], P('region', 'node'), as said below
- source_amp: float32 [8, 64, 4096], P('region', None, 'node'), may hold values from -6 to 6
- source_angle: float32 [8, 4096], P('region', 'node'), may hold values from -3.140625 to 3.140625
- impulse_taps: float32 [512, 32768], P(None, ('region', 'node'))
- incident: float32 [515, 32768], P(None, ('region', 'node')), may hold values from -6 to 6
- conductance: float32 [32768], P(('region', 'node')), may hold values from 0.5 to 2
- attach: int32 [32768], P(('region', 'node')), may hold values from 0 to 1023
- pair_slot: int32 [32, 1024], P(('region', 'node')), may hold values from 0 to 1024, as said below
- fault_node: int32 [8, 64], P('region'), may hold values from 0 to 4095
- fault_step: int32 [8, 64], P('region'), may hold values from 0 to 7
- fault_res: float32 [8, 64], P('region'), may hold values from 0.1 to 1
Outputs:
- voltages: float32 [8, 8, 64, 4096], P(None, 'region', None, 'node')
The draws below stay inside these ranges and needn't reach their ends.
Inputs may be any that keep to these rules, and one draw needn't show every extreme that they name: impedance[s] is a symmetric matrix for every s. `pair_slot`: row d (d = region index * 8 + node index) holds at position e * 32 + s, for each device e and slot s, a line end of device d paired with the one named at position d * 32 + s of row e, or 1024 where that slot is empty; a slot is filled in row d exactly when its mirror in row e is filled; each line end stands in at most one slot; in every draw some device pair fills all 32 slots.
All inputs are finite; a program needn't handle non-finite values.
Results may differ from the reference program's by a relative error of at most 0.0001.
Values sent between devices are 32-bit elements; how exact they have to be, the bound alone decides.
A program may use at most 128 MiB of HBM per device.

```python
import math
import jax
import jax.numpy as jnp
from jax import lax

SUB_ORDER = 4096
FAULT_CASES = 64
TAP_COUNT = 512
WINDOW_STEPS = 4
WINDOW_COUNT = 2
SUBS_REGION = 2
ENDS_DEV = 1024
SUBNETWORKS = 8
ROWS_DEV = 512
LOCAL_ROWS = 1024
LINE_ENDS = 32768
PAIR_SLOTS = 32
TOTAL_STEPS = 8
PAST_STEPS = 515
N_NODE = 8


def draw_impedance(key, part):
    subkeys = jax.random.split(key, SUBNETWORKS)

    def one_matrix(subkey):
        first_key, second_key = jax.random.split(subkey)
        entries = jax.random.truncated_normal(first_key, -3.0, 3.0, (SUB_ORDER, SUB_ORDER), jnp.float32)
        diagonal = jnp.exp(jax.random.uniform(second_key, (SUB_ORDER,), jnp.float32, math.log(0.5), math.log(2.0)))
        mixed = (entries + entries.T) * (0.7071 / math.sqrt(SUB_ORDER))
        row_ids = lax.iota(jnp.int32, SUB_ORDER)
        on_diag = row_ids[:, None] == row_ids[None, :]
        return jnp.where(on_diag, mixed + diagonal[:, None], mixed)
    return lax.map(one_matrix, subkeys)


def draw_impulse_taps(key, part):
    first_key, second_key = jax.random.split(key)
    lag_values = lax.iota(jnp.float32, TAP_COUNT)[:, None]
    decay_time = jnp.exp(jax.random.uniform(first_key, (1, LINE_ENDS), jnp.float32, math.log(4.0), math.log(TAP_COUNT)))
    noise = jax.random.normal(second_key, (TAP_COUNT, LINE_ENDS), jnp.float32)
    return 0.6 * noise * jnp.exp(-lag_values / decay_time) / jnp.sqrt(decay_time)


def draw_pair_slot(key, part):
    peers = LINE_ENDS // ENDS_DEV
    key_one, key_two, key_three, key_four = jax.random.split(key, 4)
    counts = jax.random.randint(key_one, (peers, peers), 0, PAIR_SLOTS + 1)
    row_ids = lax.iota(jnp.int32, peers)[:, None]
    col_ids = lax.iota(jnp.int32, peers)[None, :]
    counts = jnp.where(row_ids <= col_ids, counts, counts.T)
    first = jax.random.randint(key_two, (), 0, peers)
    second = jax.random.randint(key_three, (), 0, peers)
    forced = (row_ids == first) & (col_ids == second) | (row_ids == second) & (col_ids == first)
    counts = jnp.where(forced, PAIR_SLOTS, counts)
    slot_pos = lax.iota(jnp.int32, PAIR_SLOTS)[None, None, :]
    live = (slot_pos < counts[:, :, None]).reshape(peers, ENDS_DEV).astype(jnp.int32)
    ranks = jnp.cumsum(live, axis=1) - live

    def pick_order(subkey):
        return jax.random.permutation(subkey, ENDS_DEV).astype(jnp.int32)
    orders = jax.vmap(pick_order)(jax.random.split(key_four, peers))
    chosen = jnp.take_along_axis(orders, ranks, axis=1)
    return jnp.where(live == 1, chosen, ENDS_DEV).astype(jnp.int32)


def place_ends(array, own_key, low, top_value):
    longest = array.shape.index(max(array.shape))
    spots = []
    for shift in (0, 1):
        where = [jax.random.randint(jax.random.fold_in(own_key, axis), (), 0, length) for axis, length in enumerate(array.shape)]
        where[longest] = (where[longest] + shift) % array.shape[longest]
        spots.append(tuple(where))
    return array.at[spots[0]].set(low).at[spots[1]].set(top_value)


def block_levels(stream_key, dims, pieces, smallest, top_value):
    factor_of = 1.0
    for axis_at, parts in pieces:
        steps = jax.random.uniform(jax.random.fold_in(jax.random.fold_in(stream_key, 6), axis_at), (parts,), jnp.float32, smallest / len(pieces), top_value / len(pieces))
        factor_of = factor_of * jnp.repeat(jnp.exp(steps), dims[axis_at] // parts).reshape((-1,) + (1,) * (len(dims) - 1 - axis_at))
    return factor_of


def normal_values(rng, dims, deviation, most, shards=(), kind=jnp.bfloat16):
    array = jax.random.normal(rng, dims, jnp.float32) * deviation
    if len(shards) > 0:
        array = block_levels(rng, dims, shards, -0.22, 0.18) * array
    return jnp.clip(array, min=-most, max=most).astype(kind)


def setup_inputs(seed: int = 0) -> dict:
    key_list = jax.random.split(jax.random.key(seed), 12)
    impedance = draw_impedance(jax.random.fold_in(key_list[11], 71), 0)
    source_amp = normal_values(key_list[1], (SUBNETWORKS, FAULT_CASES, SUB_ORDER), 1.0, 6.0, ((0, 4), (2, 8)), jnp.float32)
    source_angle = jnp.clip(jax.random.uniform(key_list[2], (SUBNETWORKS, SUB_ORDER), jnp.float32, -3.140625, 3.140625), -3.140625, 3.140625)
    impulse_taps = draw_impulse_taps(jax.random.fold_in(key_list[11], 71), 0)
    incident = normal_values(key_list[4], (PAST_STEPS, LINE_ENDS), 1.0, 6.0, ((1, 32),), jnp.float32)
    conductance = jnp.clip(jnp.exp(math.log(2.0) - 1.3862944 * jax.random.uniform(key_list[5], (LINE_ENDS,), jnp.float32) ** block_levels(key_list[5], (LINE_ENDS,), ((0, 32),), -0.2, 0.2)), 0.5, 2.0)
    attach = place_ends(jax.random.randint(key_list[6], (LINE_ENDS,), 0, LOCAL_ROWS), jax.random.fold_in(key_list[6], 1), 0, LOCAL_ROWS - 1).astype(jnp.int32)
    pair_slot = draw_pair_slot(jax.random.fold_in(key_list[11], 71), 0)
    fault_node = place_ends(jax.random.randint(key_list[8], (SUBNETWORKS, FAULT_CASES), 0, SUB_ORDER), jax.random.fold_in(key_list[8], 1), 0, SUB_ORDER - 1).astype(jnp.int32)
    fault_step = place_ends(jax.random.randint(key_list[9], (SUBNETWORKS, FAULT_CASES), 0, TOTAL_STEPS), jax.random.fold_in(key_list[9], 1), 0, TOTAL_STEPS - 1).astype(jnp.int32)
    fault_res = jnp.clip(jnp.exp(math.log(1.0) - 2.3025851 * jax.random.uniform(key_list[10], (SUBNETWORKS, FAULT_CASES), jnp.float32) ** block_levels(key_list[10], (SUBNETWORKS, FAULT_CASES), ((0, 4),), -0.2, 0.2)), 0.1, 1.0)
    return dict(impedance=impedance, source_amp=source_amp, source_angle=source_angle, impulse_taps=impulse_taps, incident=incident, conductance=conductance, attach=attach, pair_slot=pair_slot, fault_node=fault_node, fault_step=fault_step, fault_res=fault_res)


omega_step = 2.0 * math.pi / 400.0


def reference(impedance, source_amp, source_angle, impulse_taps, incident, conductance, attach, pair_slot, fault_node, fault_step, fault_res):
    precise = lax.Precision.HIGHEST
    end_ids = jnp.arange(LINE_ENDS, dtype=jnp.int32)
    device = end_ids // ENDS_DEV
    subnet_of = (device // N_NODE) * SUBS_REGION + attach // ROWS_DEV
    row_of = (device % N_NODE) * ROWS_DEV + attach % ROWS_DEV
    flat_node = (subnet_of * SUB_ORDER + row_of).astype(jnp.int32)
    peers = LINE_ENDS // ENDS_DEV
    dev_grid = jnp.arange(peers, dtype=jnp.int32)[:, None]
    slot_grid = jnp.arange(ENDS_DEV, dtype=jnp.int32)[None, :]
    peer_grid = slot_grid // PAIR_SLOTS
    within = slot_grid % PAIR_SLOTS
    mirror = pair_slot[peer_grid, dev_grid * PAIR_SLOTS + within]
    valid = pair_slot < ENDS_DEV
    target = jnp.where(valid, dev_grid * ENDS_DEV + pair_slot, LINE_ENDS).reshape(-1).astype(jnp.int32)
    source_end = jnp.where(valid, peer_grid * ENDS_DEV + mirror, 0).reshape(-1).astype(jnp.int32)
    partner = jnp.zeros((LINE_ENDS,), jnp.int32).at[target].set(source_end, mode="drop")
    paired = jnp.zeros((LINE_ENDS,), jnp.int32).at[target].set(1, mode="drop") > 0
    column_index = jnp.broadcast_to(fault_node[:, None, :], (SUBNETWORKS, SUB_ORDER, FAULT_CASES))
    fault_column = jnp.transpose(jnp.take_along_axis(impedance, column_index, axis=2), (0, 2, 1))
    fault_self = jnp.take_along_axis(fault_column, fault_node[:, :, None], axis=2)[:, :, 0]
    step_total = WINDOW_STEPS * WINDOW_COUNT
    padded = jnp.concatenate([incident, jnp.zeros((step_total - WINDOW_STEPS, LINE_ENDS), jnp.float32)], axis=0)
    flipped = impulse_taps[::-1]
    base = [jnp.sum(flipped * padded[instant:instant + TAP_COUNT], axis=0) for instant in range(step_total)]
    far_list = []
    results = []
    for instant in range(step_total):
        history = jnp.broadcast_to(base[instant][None, :], (FAULT_CASES, LINE_ENDS))
        for delay_index in range(instant - WINDOW_STEPS + 1):
            history = history + impulse_taps[delay_index][None, :] * far_list[instant - WINDOW_STEPS - delay_index]
        node_hist = jax.ops.segment_sum(history.T, flat_node, num_segments=SUBNETWORKS * SUB_ORDER)
        node_hist = jnp.transpose(node_hist.reshape(SUBNETWORKS, SUB_ORDER, FAULT_CASES), (0, 2, 1))
        phase_now = jnp.cos(omega_step * instant + source_angle)
        injection = source_amp * phase_now[:, None, :] + node_hist
        open_volts = jnp.einsum("sij,scj->sci", impedance, injection, precision=precise)
        at_fault = jnp.take_along_axis(open_volts, fault_node[:, :, None], axis=2)[:, :, 0]
        current = jnp.where(fault_step <= instant, at_fault / (fault_self + fault_res), 0.0)
        voltage = open_volts - current[:, :, None] * fault_column
        results.append(voltage)
        at_ends = jnp.transpose(voltage, (1, 0, 2)).reshape(FAULT_CASES, SUBNETWORKS * SUB_ORDER)[:, flat_node]
        wave = 2.0 * conductance[None, :] * at_ends - history
        far_list.append(jnp.where(paired[None, :], wave[:, partner], 0.0))
    return jnp.stack(results)
```

```python
import math

import jax
import jax.numpy as jnp
from jax import lax
from jax.experimental import pallas as pl
from jax.experimental.pallas import tpu as pltpu
from jax.sharding import PartitionSpec as P

WINDOW_STEPS = 4
WINDOW_COUNT = 2
STEPS = WINDOW_STEPS * WINDOW_COUNT

omega_step = 2.0 * math.pi / 400.0
F32 = jnp.float32
BF16 = jnp.bfloat16


def base_kernel(taps_ref, incident_ref, base_ref, padded):
    tap_len = taps_ref.shape[0]
    past = incident_ref.shape[0]
    whole = past // 8 * 8
    padded[:whole, :] = incident_ref[:whole, :]
    padded[whole:, :] = jnp.zeros((padded.shape[0] - whole, padded.shape[1]), F32)
    padded[whole:past, :] = incident_ref[whole:past, :]

    def add_taps(block, total):
        start = pl.multiple_of(block * 8, 8)
        taps = taps_ref[pl.ds(start, 8), :]
        window = padded[pl.ds(pl.multiple_of(tap_len - 8 - start, 8), 16), :]
        for tap in range(8):
            total = total + taps[tap : tap + 1] * window[7 - tap : 15 - tap]
        return total

    base_ref[...] = lax.fori_loop(
        0, tap_len // 8, add_taps, jnp.zeros(base_ref.shape, F32), unroll=4
    )


def base_history(impulse_taps, incident):
    tap_len, ends = impulse_taps.shape
    past = incident.shape[0]
    columns = 512
    return pl.pallas_call(
        base_kernel,
        grid=(ends // columns,),
        in_specs=[
            pl.BlockSpec((tap_len, columns), lambda i: (0, i)),
            pl.BlockSpec((past, columns), lambda i: (0, i)),
        ],
        out_specs=pl.BlockSpec((STEPS, columns), lambda i: (0, i)),
        out_shape=jax.ShapeDtypeStruct((STEPS, ends), F32),
        scratch_shapes=[pltpu.VMEM(((tap_len + STEPS + 7) // 8 * 8, columns), F32)],
        compiler_params=pltpu.CompilerParams(vmem_limit_bytes=24 * 1024 * 1024),
    )(impulse_taps, incident)


def split(value):
    high = lax.reduce_precision(value, 8, 7)
    return high.astype(BF16), (value - high).astype(BF16)


def split_three(value):
    high = lax.reduce_precision(value, 8, 7)
    rest = value - high
    middle = lax.reduce_precision(rest, 8, 7)
    return high.astype(BF16), middle.astype(BF16), (rest - middle).astype(BF16)


def dot(a, b, dims):
    return lax.dot_general(a, b, dims, preferred_element_type=F32)


def exact_select(values, onehot):
    rows = values.shape[0]
    out = dot(jnp.concatenate(split_three(values), axis=0), onehot, (((1,), (0,)), ((), ())))
    return out[:rows] + out[rows : 2 * rows] + out[2 * rows :]


def grid_product(x, z_high, z_low):
    dims = (((2,), (2,)), ((0,), (0,)))
    count = x.shape[1]
    high, low = split(x)
    both = dot(jnp.concatenate([high, low], axis=1), z_high, dims)
    return both[:, :count] + both[:, count:] + dot(high, z_low, dims)


def gather_nodes(block):
    full = lax.all_gather(block, "node", axis=0, tiled=False)
    parts, subnets, count, rows = full.shape
    return jnp.transpose(full, (1, 2, 0, 3)).reshape(subnets, count, parts * rows)


def body(
    impedance,
    source_amp,
    source_angle,
    impulse_taps,
    incident,
    conductance,
    attach,
    pair_slot,
    fault_node,
    fault_step,
    fault_res,
):
    subnets, rows, order = impedance.shape
    cases = source_amp.shape[1]
    ends = impulse_taps.shape[1]
    flat = subnets * rows
    node = lax.axis_index("node")

    base = base_history(impulse_taps, incident)
    flat_ids = lax.iota(jnp.int32, flat)
    attach_map = (attach[:, None] == flat_ids[None, :]).astype(BF16)
    base_rows = exact_select(base, attach_map).reshape(STEPS, subnets, rows)
    payload = jnp.concatenate(
        [source_amp, source_angle[:, None, :], jnp.transpose(base_rows, (1, 0, 2))], axis=1
    )
    gathered = gather_nodes(payload)

    z_high, z_low = split(impedance)
    column_ids = lax.iota(jnp.int32, order)
    fault_onehot = (fault_node[:, :, None] == column_ids[None, None, :]).astype(BF16)
    batch_dims = (((2,), (2,)), ((0,), (0,)))
    fault_column = dot(fault_onehot, z_high, batch_dims) + dot(fault_onehot, z_low, batch_dims)
    own_block = lax.dynamic_slice_in_dim(impedance, node * rows, rows, axis=2)
    row_ids = lax.iota(jnp.int32, rows)
    diagonal = jnp.sum(
        jnp.where((row_ids[:, None] == row_ids[None, :])[None], own_block, 0.0), axis=2
    )
    owner_mask = fault_node[:, :, None] == (node * rows + row_ids)[None, None, :]
    self_part = jnp.sum(jnp.where(owner_mask, diagonal[:, None, :], 0.0), axis=2)
    weighted = fault_column * source_amp
    cos_part = jnp.sum(weighted * jnp.cos(source_angle)[:, None, :], axis=2)
    sin_part = jnp.sum(weighted * jnp.sin(source_angle)[:, None, :], axis=2)
    base_part = jnp.einsum(
        "scr,tsr->tsc",
        fault_column,
        base_rows,
        precision=lax.Precision.HIGHEST,
        preferred_element_type=F32,
    )
    fault_parts = lax.psum(
        jnp.concatenate([jnp.stack([self_part, cos_part, sin_part]), base_part], axis=0), "node"
    )
    denominator = fault_parts[0] + fault_res

    slot_row = pair_slot[0]
    end_ids = lax.iota(jnp.int32, ends)
    selector = end_ids[:, None] == slot_row[None, :]
    row_of_slot = jnp.sum(jnp.where(selector, attach[:, None] + 1, 0), axis=0) - 1
    slot_map = (row_of_slot[:, None] == flat_ids[None, :]).astype(BF16)
    end_values = jnp.concatenate(
        [2.0 * conductance[None, :], base[:WINDOW_STEPS], impulse_taps[:WINDOW_STEPS]], axis=0
    )
    slot_values = exact_select(end_values, selector.astype(BF16))
    slot_gain = slot_values[:1]
    slot_base = slot_values[1 : 1 + WINDOW_STEPS]
    slot_taps = slot_values[1 + WINDOW_STEPS :]

    amp = gathered[:, :cases]
    angle = gathered[:, cases : cases + 1]
    first = grid_product(
        jnp.concatenate([amp * jnp.cos(angle), amp * jnp.sin(angle), gathered[:, cases + 1 :]], axis=1),
        z_high,
        z_low,
    )
    cos_volts = first[:, :cases]
    sin_volts = first[:, cases : 2 * cases]
    base_volts = first[:, 2 * cases :]

    def source_volts(instant):
        turn = omega_step * instant
        return (
            math.cos(turn) * cos_volts
            - math.sin(turn) * sin_volts
            + base_volts[:, instant : instant + 1]
        )

    def source_fault(instant):
        turn = omega_step * instant
        return (
            math.cos(turn) * fault_parts[1]
            - math.sin(turn) * fault_parts[2]
            + fault_parts[3 + instant]
        )

    def with_fault(instant, open_volts, at_fault):
        current = jnp.where(fault_step <= instant, at_fault / denominator, 0.0)
        return open_volts - current[:, :, None] * fault_column

    results = [
        with_fault(instant, source_volts(instant), source_fault(instant))
        for instant in range(WINDOW_STEPS)
    ]
    volts = jnp.stack(results)
    by_row = jnp.transpose(volts, (0, 2, 1, 3)).reshape(WINDOW_STEPS * cases, flat)
    high, low = split(by_row)
    at_slots = dot(jnp.concatenate([high, low], axis=0), slot_map, (((1,), (1,)), ((), ())))
    at_slots = at_slots[: WINDOW_STEPS * cases] + at_slots[WINDOW_STEPS * cases :]
    outgoing = (slot_gain * at_slots).reshape(WINDOW_STEPS, cases, ends) - slot_base[:, None, :]
    incoming = lax.all_to_all(
        outgoing.reshape(WINDOW_STEPS * cases, ends),
        ("region", "node"),
        split_axis=1,
        concat_axis=1,
        tiled=True,
    ).reshape(WINDOW_STEPS, cases, ends)
    far_history = []
    for offset in range(WINDOW_STEPS):
        total = slot_taps[0][None, :] * incoming[offset]
        for delay_index in range(1, offset + 1):
            total = total + slot_taps[delay_index][None, :] * incoming[offset - delay_index]
        far_history.append(total)
    far_history = jnp.stack(far_history).reshape(WINDOW_STEPS * cases, ends)
    high, low = split(far_history)
    far_rows = dot(jnp.concatenate([high, low], axis=0), slot_map, (((1,), (0,)), ((), ())))
    far_rows = far_rows[: WINDOW_STEPS * cases] + far_rows[WINDOW_STEPS * cases :]
    far_rows = far_rows.reshape(WINDOW_STEPS * cases, subnets, rows)
    far_rows = jnp.transpose(far_rows, (1, 0, 2))
    far_fault = jnp.sum(
        far_rows.reshape(subnets, WINDOW_STEPS, cases, rows) * fault_column[:, None], axis=3
    )
    far_fault = lax.psum(jnp.transpose(far_fault, (1, 0, 2)), "node")
    second = grid_product(gather_nodes(far_rows), z_high, z_low)
    second = second.reshape(subnets, WINDOW_STEPS, cases, rows)
    for offset in range(WINDOW_STEPS):
        instant = WINDOW_STEPS + offset
        results.append(
            with_fault(
                instant,
                source_volts(instant) + second[:, offset],
                source_fault(instant) + far_fault[offset],
            )
        )
    return jnp.stack(results)


def solution(mesh):
    in_specs = (
        P("region", "node", None),
        P("region", None, "node"),
        P("region", "node"),
        P(None, ("region", "node")),
        P(None, ("region", "node")),
        P(("region", "node")),
        P(("region", "node")),
        P(("region", "node"), None),
        P("region", None),
        P("region", None),
        P("region", None),
    )
    out_specs = P(None, "region", None, "node")
    return jax.shard_map(body, mesh=mesh, in_specs=in_specs, out_specs=out_specs, check_vma=False)
```

```python
import functools
import math

import jax
import jax.numpy as jnp
from jax import lax
from jax.experimental import pallas as pl
from jax.experimental.pallas import tpu as pltpu
from jax.sharding import PartitionSpec as P

WINDOW_STEPS = 4
WINDOW_COUNT = 2
STEPS = WINDOW_STEPS * WINDOW_COUNT

omega_step = 2.0 * math.pi / 400.0
F32 = jnp.float32
BF16 = jnp.bfloat16


def base_kernel(taps_ref, incident_ref, base_ref, padded):
    tap_len = taps_ref.shape[0]
    past = incident_ref.shape[0]
    whole = past // 8 * 8
    padded[:whole, :] = incident_ref[:whole, :]
    padded[whole:, :] = jnp.zeros((padded.shape[0] - whole, padded.shape[1]), F32)
    padded[whole:past, :] = incident_ref[whole:past, :]

    def add_taps(block, total):
        start = pl.multiple_of(block * 8, 8)
        taps = taps_ref[pl.ds(start, 8), :]
        window = padded[pl.ds(pl.multiple_of(tap_len - 8 - start, 8), 16), :]
        for tap in range(8):
            total = total + taps[tap : tap + 1] * window[7 - tap : 15 - tap]
        return total

    base_ref[...] = lax.fori_loop(
        0, tap_len // 8, add_taps, jnp.zeros(base_ref.shape, F32), unroll=4
    )


def base_history(impulse_taps, incident):
    tap_len, ends = impulse_taps.shape
    past = incident.shape[0]
    columns = 512
    return pl.pallas_call(
        base_kernel,
        grid=(ends // columns,),
        in_specs=[
            pl.BlockSpec((tap_len, columns), lambda i: (0, i)),
            pl.BlockSpec((past, columns), lambda i: (0, i)),
        ],
        out_specs=pl.BlockSpec((STEPS, columns), lambda i: (0, i)),
        out_shape=jax.ShapeDtypeStruct((STEPS, ends), F32),
        scratch_shapes=[pltpu.VMEM(((tap_len + STEPS + 7) // 8 * 8, columns), F32)],
        compiler_params=pltpu.CompilerParams(vmem_limit_bytes=24 * 1024 * 1024),
    )(impulse_taps, incident)


def split(value):
    high = lax.reduce_precision(value, 8, 7)
    return high.astype(BF16), (value - high).astype(BF16)


def split_three(value):
    high = lax.reduce_precision(value, 8, 7)
    rest = value - high
    middle = lax.reduce_precision(rest, 8, 7)
    return high.astype(BF16), middle.astype(BF16), (rest - middle).astype(BF16)


def dot(a, b, dims):
    return lax.dot_general(a, b, dims, preferred_element_type=F32)


NT = (((1,), (1,)), ((), ()))


def exact_select(values, onehot):
    rows = values.shape[0]
    out = dot(jnp.concatenate(split_three(values), axis=0), onehot, (((1,), (0,)), ((), ())))
    return out[:rows] + out[rows : 2 * rows] + out[2 * rows :]


def select_rows(values, slot_map):
    rows = values.shape[0]
    out = dot(jnp.concatenate(split(values), axis=0), slot_map, NT)
    return out[:rows] + out[rows:]


def pieces(value):
    high = value.astype(BF16)
    return high, (value - high.astype(F32)).astype(BF16)


def block_product(x, z):
    count = x.shape[0]
    x_high, x_low = pieces(x)
    z_high, z_low = pieces(z)
    both = dot(jnp.concatenate([x_high, x_low], axis=0), z_high, NT)
    return both[:count] + both[count:] + dot(x_high, z_low, NT)


def accumulate(out_ref, index, first, value):
    @pl.when(first)
    def _():
        out_ref[index] = value

    @pl.when(jnp.logical_not(first))
    def _():
        out_ref[index] += value


def column_kernel(fault_ref, z_ref, out_ref):
    part = pl.program_id(1)
    cases = fault_ref.shape[1]
    depth = z_ref.shape[2]
    ids = lax.broadcasted_iota(jnp.int32, (cases, depth), 1) + part * depth
    onehot = jnp.where(fault_ref[0] == ids, 1.0, 0.0).astype(BF16)
    z_high, z_low = pieces(z_ref[0])
    value = dot(onehot, z_high, NT) + dot(onehot, z_low, NT)
    accumulate(out_ref, 0, part == 0, value)


def fault_columns(fault_node, impedance, parts):
    subnets, rows, order = impedance.shape
    cases = fault_node.shape[1]
    depth = order // parts
    return pl.pallas_call(
        column_kernel,
        grid=(subnets, parts),
        in_specs=[
            pl.BlockSpec((1, cases, 1), lambda s, n: (s, 0, 0)),
            pl.BlockSpec((1, rows, depth), lambda s, n: (s, 0, n)),
        ],
        out_specs=pl.BlockSpec((1, cases, rows), lambda s, n: (s, 0, 0)),
        out_shape=jax.ShapeDtypeStruct((subnets, cases, rows), F32),
        compiler_params=pltpu.CompilerParams(vmem_limit_bytes=24 * 1024 * 1024),
    )(fault_node[:, :, None], impedance)


def source_kernel(cases, x_ref, z_ref, out_ref):
    amp = x_ref[0, 0, :cases, :]
    hist = x_ref[0, 0, cases : cases + STEPS, :]
    angle = x_ref[0, 0, cases + STEPS : cases + STEPS + 1, :]
    x = jnp.concatenate([amp * jnp.cos(angle), amp * jnp.sin(angle), hist], axis=0)
    accumulate(out_ref, 0, pl.program_id(1) == 0, block_product(x, z_ref[0]))


def source_product(gathered, impedance, cases):
    parts, subnets, count, depth = gathered.shape
    rows = impedance.shape[1]
    total = 2 * cases + STEPS
    return pl.pallas_call(
        functools.partial(source_kernel, cases),
        grid=(subnets, parts),
        in_specs=[
            pl.BlockSpec((1, 1, count, depth), lambda s, n: (n, s, 0, 0)),
            pl.BlockSpec((1, rows, depth), lambda s, n: (s, 0, n)),
        ],
        out_specs=pl.BlockSpec((1, total, rows), lambda s, n: (s, 0, 0)),
        out_shape=jax.ShapeDtypeStruct((subnets, total, rows), F32),
        compiler_params=pltpu.CompilerParams(vmem_limit_bytes=24 * 1024 * 1024),
    )(gathered, impedance)


def far_waves(volts, column, currents):
    cases = currents[0][0].shape[-2]
    cos_wave = volts[..., :cases, :]
    sin_wave = volts[..., cases : 2 * cases, :]
    fault_wave = column[..., :cases, :]
    second_subnet = column[..., cases : cases + 1, :] > 0.5
    waves = []
    for instant in range(WINDOW_STEPS):
        turn = omega_step * instant
        free = volts[..., 2 * cases + instant : 2 * cases + instant + 1, :]
        current = jnp.where(second_subnet, currents[instant][1], currents[instant][0])
        waves.append(
            math.cos(turn) * cos_wave - math.sin(turn) * sin_wave + free - current * fault_wave
        )
    return waves


def far_history(waves, taps):
    history = []
    for offset in range(WINDOW_STEPS):
        total = taps[0] * waves[offset]
        for delay_index in range(1, offset + 1):
            total = total + taps[delay_index] * waves[offset - delay_index]
        history.append(total)
    return history


def far_kernel(volts_ref, column_ref, slot_ref, current_ref, z_ref, out_ref, high, low):
    first = pl.program_id(0) == 0
    sources = volts_ref.shape[0]
    lanes = volts_ref.shape[3]
    subnets, rows, depth = z_ref.shape
    flat = subnets * depth
    currents = [[current_ref[t, s] for s in range(subnets)] for t in range(WINDOW_STEPS)]
    slot_rows = []
    for source in range(sources):
        taps = [slot_ref[0, source, j : j + 1, :] for j in range(WINDOW_STEPS)]
        slot_rows.append(slot_ref[0, source, WINDOW_STEPS : WINDOW_STEPS + 1, :])
        waves = far_waves(volts_ref[source, 0], column_ref[source, 0], currents)
        history = jnp.concatenate(far_history(waves, taps), axis=0)
        one, two = pieces(history)
        high[:, source * lanes : (source + 1) * lanes] = one
        low[:, source * lanes : (source + 1) * lanes] = two
    slot_row = jnp.concatenate(slot_rows, axis=1).astype(jnp.int32)
    ids = lax.broadcasted_iota(jnp.int32, (flat, slot_row.shape[1]), 0)
    onehot = jnp.where(ids == slot_row, 1.0, 0.0).astype(BF16)
    injected = dot(high[...], onehot, NT) + dot(low[...], onehot, NT)
    for subnet in range(subnets):
        x = injected[:, subnet * depth : (subnet + 1) * depth]
        accumulate(out_ref, subnet, first, block_product(x, z_ref[subnet]))


def far_product(volts, column, slots, currents, impedance):
    sources, parts, volt_rows, lanes = volts.shape
    column_rows = column.shape[2]
    subnets, rows, order = impedance.shape
    cases = currents.shape[2]
    depth = order // parts
    total = WINDOW_STEPS * cases
    return pl.pallas_call(
        far_kernel,
        grid=(parts,),
        in_specs=[
            pl.BlockSpec((sources, 1, volt_rows, lanes), lambda n: (0, n, 0, 0)),
            pl.BlockSpec((sources, 1, column_rows, lanes), lambda n: (0, n, 0, 0)),
            pl.BlockSpec((1,) + slots.shape[1:], lambda n: (n, 0, 0, 0)),
            pl.BlockSpec(currents.shape, lambda n: (0, 0, 0, 0)),
            pl.BlockSpec((subnets, rows, depth), lambda n: (0, 0, n)),
        ],
        out_specs=pl.BlockSpec((subnets, total, rows), lambda n: (0, 0, 0)),
        out_shape=jax.ShapeDtypeStruct((subnets, total, rows), F32),
        scratch_shapes=[
            pltpu.VMEM((total, sources * lanes), BF16),
            pltpu.VMEM((total, sources * lanes), BF16),
        ],
        compiler_params=pltpu.CompilerParams(vmem_limit_bytes=44 * 1024 * 1024),
    )(volts, column, slots, currents, impedance)


def body(
    regions,
    nodes,
    impedance,
    source_amp,
    source_angle,
    impulse_taps,
    incident,
    conductance,
    attach,
    pair_slot,
    fault_node,
    fault_step,
    fault_res,
):
    subnets, rows, order = impedance.shape
    cases = source_amp.shape[1]
    ends = impulse_taps.shape[1]
    slots = ends // (regions * nodes)
    lanes = regions * slots
    flat = subnets * rows
    node = lax.axis_index("node")
    region = lax.axis_index("region")

    base = base_history(impulse_taps, incident)
    flat_ids = lax.iota(jnp.int32, flat)
    attach_map = (attach[:, None] == flat_ids[None, :]).astype(BF16)
    base_rows = exact_select(base, attach_map).reshape(STEPS, subnets, rows)
    payload = jnp.concatenate(
        [source_amp, jnp.transpose(base_rows, (1, 0, 2)), source_angle[:, None, :]], axis=1
    )
    gathered = lax.all_gather(payload, "node", axis=0, tiled=False)

    slot_row = pair_slot[0]
    end_ids = lax.iota(jnp.int32, ends)
    selector = end_ids[:, None] == slot_row[None, :]
    row_of_slot = jnp.sum(jnp.where(selector, attach[:, None] + 1, 0), axis=0) - 1
    slot_map = (row_of_slot[:, None] == flat_ids[None, :]).astype(BF16)
    end_values = jnp.concatenate(
        [2.0 * conductance[None, :], base[:WINDOW_STEPS], impulse_taps[:WINDOW_STEPS]], axis=0
    )
    slot_values = exact_select(end_values, selector.astype(BF16))
    slot_gain = slot_values[:1]
    slot_base = slot_values[1 : 1 + WINDOW_STEPS]
    slot_info = jnp.concatenate(
        [slot_values[1 + WINDOW_STEPS :], row_of_slot.astype(F32)[None, :]], axis=0
    )
    info_rows = slot_info.shape[0]
    own_info = jnp.transpose(
        slot_info.reshape(info_rows, regions, nodes, slots), (2, 0, 1, 3)
    ).reshape(nodes, info_rows, lanes)
    all_info = lax.all_gather(own_info, "node", axis=0, tiled=False)

    def to_region(block):
        count = block.shape[0]
        block = lax.all_to_all(block, "region", split_axis=1, concat_axis=1, tiled=True)
        block = block.reshape(count, regions, nodes, slots)
        block = jnp.transpose(block, (2, 0, 1, 3)).reshape(nodes, count, lanes)
        return lax.all_gather(block, "node", axis=0, tiled=False)

    def by_flat(block):
        return jnp.transpose(block, (1, 0, 2)).reshape(block.shape[1], flat)

    fault_column = fault_columns(fault_node, impedance, nodes)
    column_slots = select_rows(by_flat(fault_column), slot_map)
    subnet_of_slot = (row_of_slot >= rows).astype(F32)[None, :]
    column_all = to_region(jnp.concatenate([slot_gain * column_slots, subnet_of_slot], axis=0))

    own_block = lax.dynamic_slice_in_dim(impedance, node * rows, rows, axis=2)
    row_ids = lax.iota(jnp.int32, rows)
    diagonal = jnp.sum(
        jnp.where((row_ids[:, None] == row_ids[None, :])[None], own_block, 0.0), axis=2
    )
    owner_mask = fault_node[:, :, None] == (node * rows + row_ids)[None, None, :]
    self_part = jnp.sum(jnp.where(owner_mask, diagonal[:, None, :], 0.0), axis=2)
    weighted = fault_column * source_amp
    cos_part = jnp.sum(weighted * jnp.cos(source_angle)[:, None, :], axis=2)
    sin_part = jnp.sum(weighted * jnp.sin(source_angle)[:, None, :], axis=2)
    base_part = jnp.einsum(
        "scr,tsr->tsc",
        fault_column,
        base_rows,
        precision=lax.Precision.HIGHEST,
        preferred_element_type=F32,
    )
    own_parts = jnp.concatenate(
        [
            jnp.stack([self_part, cos_part, sin_part]),
            base_part,
            jnp.stack([fault_res, fault_step.astype(F32)]),
        ],
        axis=0,
    )
    all_parts = lax.all_gather(own_parts, ("region", "node"), axis=0, tiled=False)
    all_parts = all_parts.reshape((regions, nodes) + own_parts.shape)
    sums = jnp.sum(all_parts[:, :, : 3 + STEPS], axis=1)
    denominators = sums[:, 0] + all_parts[:, 0, 3 + STEPS]
    starts = all_parts[:, 0, 4 + STEPS]

    def source_fault(sums, instant):
        turn = omega_step * instant
        return (
            math.cos(turn) * sums[..., 1, :, :]
            - math.sin(turn) * sums[..., 2, :, :]
            + sums[..., 3 + instant, :, :]
        )

    currents = jnp.stack(
        [
            jnp.where(starts <= instant, source_fault(sums, instant) / denominators, 0.0)
            for instant in range(WINDOW_STEPS)
        ]
    )
    currents = jnp.transpose(currents, (0, 2, 3, 1))
    currents = jnp.broadcast_to(currents[..., None], currents.shape + (slots,))
    currents = currents.reshape(WINDOW_STEPS, subnets, cases, lanes)
    own_sums = lax.dynamic_index_in_dim(sums, region, axis=0, keepdims=False)
    denominator = own_sums[0] + fault_res

    first = source_product(gathered, impedance, cases)
    cos_volts = first[:, :cases]
    sin_volts = first[:, cases : 2 * cases]
    base_volts = first[:, 2 * cases :]
    volt_slots = slot_gain * select_rows(by_flat(first[:, : 2 * cases + WINDOW_STEPS]), slot_map)
    volts_all = to_region(
        jnp.concatenate([volt_slots[: 2 * cases], volt_slots[2 * cases :] - slot_base], axis=0)
    )

    info_own = jnp.transpose(own_info, (1, 0, 2))
    waves = far_waves(
        lax.dynamic_index_in_dim(volts_all, node, axis=1, keepdims=False),
        lax.dynamic_index_in_dim(column_all, node, axis=1, keepdims=False),
        [[currents[t, s][None] for s in range(subnets)] for t in range(WINDOW_STEPS)],
    )
    own_history = far_history(waves, [info_own[j][:, None, :] for j in range(WINDOW_STEPS)])
    own_column = jnp.transpose(
        column_slots.reshape(cases, regions, nodes, slots), (2, 0, 1, 3)
    ).reshape(nodes, cases, lanes)
    own_rows = info_own[WINDOW_STEPS][:, None, :]
    far_part = jnp.stack(
        [
            jnp.stack(
                [
                    jnp.sum(
                        jnp.where((own_rows >= s * rows) & (own_rows < (s + 1) * rows), h * own_column, 0.0),
                        axis=(0, 2),
                    )
                    for s in range(subnets)
                ]
            )
            for h in own_history
        ]
    )
    far_fault = jnp.sum(lax.all_gather(far_part, "node", axis=0, tiled=False), axis=0)
    second = far_product(volts_all, column_all, all_info, currents, impedance)
    second = second.reshape(subnets, WINDOW_STEPS, cases, rows)

    results = []
    for instant in range(STEPS):
        turn = omega_step * instant
        open_volts = (
            math.cos(turn) * cos_volts
            - math.sin(turn) * sin_volts
            + base_volts[:, instant : instant + 1]
        )
        at_fault = source_fault(own_sums, instant)
        if instant >= WINDOW_STEPS:
            open_volts = open_volts + second[:, instant - WINDOW_STEPS]
            at_fault = at_fault + far_fault[instant - WINDOW_STEPS]
        current = jnp.where(fault_step <= instant, at_fault / denominator, 0.0)
        results.append(open_volts - current[:, :, None] * fault_column)
    return jnp.stack(results)


def solution(mesh):
    in_specs = (
        P("region", "node", None),
        P("region", None, "node"),
        P("region", "node"),
        P(None, ("region", "node")),
        P(None, ("region", "node")),
        P(("region", "node")),
        P(("region", "node")),
        P(("region", "node"), None),
        P("region", None),
        P("region", None),
        P("region", None),
    )
    out_specs = P(None, "region", None, "node")
    return jax.shard_map(
        functools.partial(body, mesh.shape["region"], mesh.shape["node"]),
        mesh=mesh,
        in_specs=in_specs,
        out_specs=out_specs,
        check_vma=False,
    )
```

```python
import functools
import math

import jax
import jax.numpy as jnp
from jax import lax
from jax.experimental import pallas as pl
from jax.experimental.pallas import tpu as pltpu
from jax.sharding import PartitionSpec as P

WINDOW_STEPS = 4
WINDOW_COUNT = 2
STEPS = WINDOW_STEPS * WINDOW_COUNT

omega_step = 2.0 * math.pi / 400.0
F32 = jnp.float32
BF16 = jnp.bfloat16


def base_kernel(taps_ref, incident_ref, base_ref, padded):
    tap_len = taps_ref.shape[0]
    past = incident_ref.shape[0]
    whole = past // 8 * 8
    padded[:whole, :] = incident_ref[:whole, :]
    padded[whole:, :] = jnp.zeros((padded.shape[0] - whole, padded.shape[1]), F32)
    padded[whole:past, :] = incident_ref[whole:past, :]

    def add_taps(block, total):
        start = pl.multiple_of(block * 8, 8)
        taps = taps_ref[pl.ds(start, 8), :]
        window = padded[pl.ds(pl.multiple_of(tap_len - 8 - start, 8), 16), :]
        for tap in range(8):
            total = total + taps[tap : tap + 1] * window[7 - tap : 15 - tap]
        return total

    base_ref[...] = lax.fori_loop(
        0, tap_len // 8, add_taps, jnp.zeros(base_ref.shape, F32), unroll=4
    )


def base_history(impulse_taps, incident):
    tap_len, ends = impulse_taps.shape
    past = incident.shape[0]
    columns = 512
    return pl.pallas_call(
        base_kernel,
        grid=(ends // columns,),
        in_specs=[
            pl.BlockSpec((tap_len, columns), lambda i: (0, i)),
            pl.BlockSpec((past, columns), lambda i: (0, i)),
        ],
        out_specs=pl.BlockSpec((STEPS, columns), lambda i: (0, i)),
        out_shape=jax.ShapeDtypeStruct((STEPS, ends), F32),
        scratch_shapes=[pltpu.VMEM(((tap_len + STEPS + 7) // 8 * 8, columns), F32)],
        compiler_params=pltpu.CompilerParams(vmem_limit_bytes=24 * 1024 * 1024),
    )(impulse_taps, incident)


def split(value):
    high = lax.reduce_precision(value, 8, 7)
    return high.astype(BF16), (value - high).astype(BF16)


def split_three(value):
    high = lax.reduce_precision(value, 8, 7)
    rest = value - high
    middle = lax.reduce_precision(rest, 8, 7)
    return high.astype(BF16), middle.astype(BF16), (rest - middle).astype(BF16)


def dot(a, b, dims):
    return lax.dot_general(a, b, dims, preferred_element_type=F32)


NT = (((1,), (1,)), ((), ()))


def exact_select(values, onehot):
    rows = values.shape[0]
    out = dot(jnp.concatenate(split_three(values), axis=0), onehot, (((1,), (0,)), ((), ())))
    return out[:rows] + out[rows : 2 * rows] + out[2 * rows :]


def select_rows(values, slot_map):
    rows = values.shape[0]
    out = dot(jnp.concatenate(split(values), axis=0), slot_map, NT)
    return out[:rows] + out[rows:]


def pieces(value):
    high = value.astype(BF16)
    return high, (value - high.astype(F32)).astype(BF16)


def block_product(x, z):
    count = x.shape[0]
    x_high, x_low = pieces(x)
    z_high, z_low = pieces(z)
    both = dot(jnp.concatenate([x_high, x_low], axis=0), z_high, NT)
    return both[:count] + both[count:] + dot(x_high, z_low, NT)


def accumulate(out_ref, index, first, value):
    @pl.when(first)
    def _():
        out_ref[index] = value

    @pl.when(jnp.logical_not(first))
    def _():
        out_ref[index] += value


def column_kernel(fault_ref, z_ref, out_ref):
    part = pl.program_id(1)
    cases = fault_ref.shape[1]
    depth = z_ref.shape[2]
    ids = lax.broadcasted_iota(jnp.int32, (cases, depth), 1) + part * depth
    onehot = jnp.where(fault_ref[0] == ids, 1.0, 0.0).astype(BF16)
    z_high, z_low = pieces(z_ref[0])
    value = dot(onehot, z_high, NT) + dot(onehot, z_low, NT)
    accumulate(out_ref, 0, part == 0, value)


def fault_columns(fault_node, impedance, parts):
    subnets, rows, order = impedance.shape
    cases = fault_node.shape[1]
    depth = order // parts
    return pl.pallas_call(
        column_kernel,
        grid=(subnets, parts),
        in_specs=[
            pl.BlockSpec((1, cases, 1), lambda s, n: (s, 0, 0)),
            pl.BlockSpec((1, rows, depth), lambda s, n: (s, 0, n)),
        ],
        out_specs=pl.BlockSpec((1, cases, rows), lambda s, n: (s, 0, 0)),
        out_shape=jax.ShapeDtypeStruct((subnets, cases, rows), F32),
        compiler_params=pltpu.CompilerParams(vmem_limit_bytes=52 * 1024 * 1024),
    )(fault_node[:, :, None], impedance)


def source_kernel(cases, x_ref, z_ref, out_ref):
    amp = x_ref[0, 0, :cases, :]
    hist = x_ref[0, 0, cases : cases + STEPS, :]
    angle = x_ref[0, 0, cases + STEPS : cases + STEPS + 1, :]
    x = jnp.concatenate([amp * jnp.cos(angle), amp * jnp.sin(angle), hist], axis=0)
    accumulate(out_ref, 0, pl.program_id(1) == 0, block_product(x, z_ref[0]))


def source_product(gathered, impedance, cases):
    parts, subnets, count, depth = gathered.shape
    rows = impedance.shape[1]
    total = 2 * cases + STEPS
    return pl.pallas_call(
        functools.partial(source_kernel, cases),
        grid=(subnets, parts),
        in_specs=[
            pl.BlockSpec((1, 1, count, depth), lambda s, n: (n, s, 0, 0)),
            pl.BlockSpec((1, rows, depth), lambda s, n: (s, 0, n)),
        ],
        out_specs=pl.BlockSpec((1, total, rows), lambda s, n: (s, 0, 0)),
        out_shape=jax.ShapeDtypeStruct((subnets, total, rows), F32),
        compiler_params=pltpu.CompilerParams(vmem_limit_bytes=52 * 1024 * 1024),
    )(gathered, impedance)


def far_waves(volts, column, currents):
    cases = currents[0][0].shape[-2]
    cos_wave = volts[..., :cases, :]
    sin_wave = volts[..., cases : 2 * cases, :]
    fault_wave = column[..., :cases, :]
    second_subnet = column[..., cases : cases + 1, :] > 0.5
    waves = []
    for instant in range(WINDOW_STEPS):
        turn = omega_step * instant
        free = volts[..., 2 * cases + instant : 2 * cases + instant + 1, :]
        current = jnp.where(second_subnet, currents[instant][1], currents[instant][0])
        waves.append(
            math.cos(turn) * cos_wave - math.sin(turn) * sin_wave + free - current * fault_wave
        )
    return waves


def far_history(waves, taps):
    history = []
    for offset in range(WINDOW_STEPS):
        total = taps[0] * waves[offset]
        for delay_index in range(1, offset + 1):
            total = total + taps[delay_index] * waves[offset - delay_index]
        history.append(total)
    return history


def far_kernel(volts_ref, column_ref, slot_ref, current_ref, z_ref, out_ref, high, low):
    first = pl.program_id(0) == 0
    sources = volts_ref.shape[0]
    lanes = volts_ref.shape[3]
    subnets, rows, depth = z_ref.shape
    flat = subnets * depth
    currents = [[current_ref[t, s] for s in range(subnets)] for t in range(WINDOW_STEPS)]
    slot_rows = []
    for source in range(sources):
        taps = [slot_ref[0, source, j : j + 1, :] for j in range(WINDOW_STEPS)]
        slot_rows.append(slot_ref[0, source, WINDOW_STEPS : WINDOW_STEPS + 1, :])
        waves = far_waves(volts_ref[source, 0], column_ref[source, 0], currents)
        history = jnp.concatenate(far_history(waves, taps), axis=0)
        one, two = pieces(history)
        high[:, source * lanes : (source + 1) * lanes] = one
        low[:, source * lanes : (source + 1) * lanes] = two
    slot_row = jnp.concatenate(slot_rows, axis=1).astype(jnp.int32)
    ids = lax.broadcasted_iota(jnp.int32, (flat, slot_row.shape[1]), 0)
    onehot = jnp.where(ids == slot_row, 1.0, 0.0).astype(BF16)
    injected = dot(high[...], onehot, NT) + dot(low[...], onehot, NT)
    for subnet in range(subnets):
        x = injected[:, subnet * depth : (subnet + 1) * depth]
        accumulate(out_ref, subnet, first, block_product(x, z_ref[subnet]))


def far_product(volts, column, slots, currents, impedance):
    sources, parts, volt_rows, lanes = volts.shape
    column_rows = column.shape[2]
    subnets, rows, order = impedance.shape
    cases = currents.shape[2]
    depth = order // parts
    total = WINDOW_STEPS * cases
    return pl.pallas_call(
        far_kernel,
        grid=(parts,),
        in_specs=[
            pl.BlockSpec((sources, 1, volt_rows, lanes), lambda n: (0, n, 0, 0)),
            pl.BlockSpec((sources, 1, column_rows, lanes), lambda n: (0, n, 0, 0)),
            pl.BlockSpec((1,) + slots.shape[1:], lambda n: (n, 0, 0, 0)),
            pl.BlockSpec(currents.shape, lambda n: (0, 0, 0, 0)),
            pl.BlockSpec((subnets, rows, depth), lambda n: (0, 0, n)),
        ],
        out_specs=pl.BlockSpec((subnets, total, rows), lambda n: (0, 0, 0)),
        out_shape=jax.ShapeDtypeStruct((subnets, total, rows), F32),
        scratch_shapes=[
            pltpu.VMEM((total, sources * lanes), BF16),
            pltpu.VMEM((total, sources * lanes), BF16),
        ],
        compiler_params=pltpu.CompilerParams(vmem_limit_bytes=52 * 1024 * 1024),
        cost_estimate=pl.CostEstimate(
            flops=6 * parts * total * rows * depth * subnets + 4 * parts * total * sources * lanes * subnets * depth,
            bytes_accessed=4 * (impedance.size + volts.size + column.size),
            transcendentals=0,
        ),
    )(volts, column, slots, currents, impedance)


def body(
    regions,
    nodes,
    impedance,
    source_amp,
    source_angle,
    impulse_taps,
    incident,
    conductance,
    attach,
    pair_slot,
    fault_node,
    fault_step,
    fault_res,
):
    subnets, rows, order = impedance.shape
    cases = source_amp.shape[1]
    ends = impulse_taps.shape[1]
    slots = ends // (regions * nodes)
    lanes = regions * slots
    flat = subnets * rows
    node = lax.axis_index("node")
    region = lax.axis_index("region")

    base = base_history(impulse_taps, incident)
    flat_ids = lax.iota(jnp.int32, flat)
    attach_map = (attach[:, None] == flat_ids[None, :]).astype(BF16)
    base_rows = exact_select(base, attach_map).reshape(STEPS, subnets, rows)
    payload = jnp.concatenate(
        [source_amp, jnp.transpose(base_rows, (1, 0, 2)), source_angle[:, None, :]], axis=1
    )
    gathered = lax.all_gather(payload, "node", axis=0, tiled=False)

    slot_row = pair_slot[0]
    end_ids = lax.iota(jnp.int32, ends)
    selector = end_ids[:, None] == slot_row[None, :]
    row_of_slot = jnp.sum(jnp.where(selector, attach[:, None] + 1, 0), axis=0) - 1
    slot_map = (row_of_slot[:, None] == flat_ids[None, :]).astype(BF16)
    end_values = jnp.concatenate(
        [2.0 * conductance[None, :], base[:WINDOW_STEPS], impulse_taps[:WINDOW_STEPS]], axis=0
    )
    slot_values = exact_select(end_values, selector.astype(BF16))
    slot_gain = slot_values[:1]
    slot_base = slot_values[1 : 1 + WINDOW_STEPS]
    slot_info = jnp.concatenate(
        [slot_values[1 + WINDOW_STEPS :], row_of_slot.astype(F32)[None, :]], axis=0
    )
    info_rows = slot_info.shape[0]
    own_info = jnp.transpose(
        slot_info.reshape(info_rows, regions, nodes, slots), (2, 0, 1, 3)
    ).reshape(nodes, info_rows, lanes)

    def to_region(block, more=None):
        count = block.shape[0]
        block = lax.all_to_all(block, "region", split_axis=1, concat_axis=1, tiled=True)
        block = block.reshape(count, regions, nodes, slots)
        block = jnp.transpose(block, (2, 0, 1, 3)).reshape(nodes, count, lanes)
        if more is not None:
            block = jnp.concatenate([block, more], axis=1)
        block = jnp.pad(block, ((0, 0), (0, -block.shape[1] % 8), (0, 0)))
        return lax.all_gather(block, "node", axis=0, tiled=False)

    def by_flat(block):
        return jnp.transpose(block, (1, 0, 2)).reshape(block.shape[1], flat)

    fault_column = fault_columns(fault_node, impedance, nodes)
    column_slots = select_rows(by_flat(fault_column), slot_map)
    subnet_of_slot = (row_of_slot >= rows).astype(F32)[None, :]

    own_block = lax.dynamic_slice_in_dim(impedance, node * rows, rows, axis=2)
    row_ids = lax.iota(jnp.int32, rows)
    diagonal = jnp.sum(
        jnp.where((row_ids[:, None] == row_ids[None, :])[None], own_block, 0.0), axis=2
    )
    owner_mask = fault_node[:, :, None] == (node * rows + row_ids)[None, None, :]
    self_part = jnp.sum(jnp.where(owner_mask, diagonal[:, None, :], 0.0), axis=2)
    weighted = fault_column * source_amp
    cos_part = jnp.sum(weighted * jnp.cos(source_angle)[:, None, :], axis=2)
    sin_part = jnp.sum(weighted * jnp.sin(source_angle)[:, None, :], axis=2)
    base_part = jnp.einsum(
        "scr,tsr->tsc",
        fault_column,
        base_rows,
        precision=lax.Precision.HIGHEST,
        preferred_element_type=F32,
    )
    own_parts = jnp.concatenate(
        [
            jnp.stack([self_part, cos_part, sin_part]),
            base_part,
            jnp.stack([fault_res, fault_step.astype(F32)]),
        ],
        axis=0,
    )
    part_lanes = nodes * slots
    part_rows = -(-own_parts.size // part_lanes)
    part_block = jnp.pad(own_parts.reshape(-1), (0, part_rows * part_lanes - own_parts.size))
    part_block = jnp.broadcast_to(
        part_block.reshape(part_rows, 1, part_lanes), (part_rows, regions, part_lanes)
    ).reshape(part_rows, ends)
    column_count = cases + 1 + part_rows
    column_all = to_region(
        jnp.concatenate([slot_gain * column_slots, subnet_of_slot, part_block], axis=0), own_info
    )
    all_info = column_all[:, :, column_count : column_count + info_rows]
    all_parts = column_all[:, :, cases + 1 : column_count].reshape(
        nodes, nodes, part_rows, regions, slots
    )
    all_parts = jnp.transpose(all_parts, (3, 0, 2, 1, 4)).reshape(regions, nodes, -1)
    all_parts = all_parts[:, :, : own_parts.size].reshape((regions, nodes) + own_parts.shape)
    sums = jnp.sum(all_parts[:, :, : 3 + STEPS], axis=1)
    denominators = sums[:, 0] + all_parts[:, 0, 3 + STEPS]
    starts = all_parts[:, 0, 4 + STEPS]

    def source_fault(sums, instant):
        turn = omega_step * instant
        return (
            math.cos(turn) * sums[..., 1, :, :]
            - math.sin(turn) * sums[..., 2, :, :]
            + sums[..., 3 + instant, :, :]
        )

    currents = jnp.stack(
        [
            jnp.where(starts <= instant, source_fault(sums, instant) / denominators, 0.0)
            for instant in range(WINDOW_STEPS)
        ]
    )
    currents = jnp.transpose(currents, (0, 2, 3, 1))
    currents = jnp.broadcast_to(currents[..., None], currents.shape + (slots,))
    currents = currents.reshape(WINDOW_STEPS, subnets, cases, lanes)
    own_sums = lax.dynamic_index_in_dim(sums, region, axis=0, keepdims=False)
    denominator = own_sums[0] + fault_res

    first = source_product(gathered, impedance, cases)
    cos_volts = first[:, :cases]
    sin_volts = first[:, cases : 2 * cases]
    base_volts = first[:, 2 * cases :]
    volt_slots = slot_gain * select_rows(by_flat(first[:, : 2 * cases + WINDOW_STEPS]), slot_map)
    volts_all = to_region(
        jnp.concatenate([volt_slots[: 2 * cases], volt_slots[2 * cases :] - slot_base], axis=0)
    )

    info_own = jnp.transpose(own_info, (1, 0, 2))
    waves = far_waves(
        lax.dynamic_index_in_dim(volts_all, node, axis=1, keepdims=False),
        lax.dynamic_index_in_dim(column_all, node, axis=1, keepdims=False),
        [[currents[t, s][None] for s in range(subnets)] for t in range(WINDOW_STEPS)],
    )
    own_history = far_history(waves, [info_own[j][:, None, :] for j in range(WINDOW_STEPS)])
    own_column = jnp.transpose(
        column_slots.reshape(cases, regions, nodes, slots), (2, 0, 1, 3)
    ).reshape(nodes, cases, lanes)
    own_rows = info_own[WINDOW_STEPS][:, None, :]
    far_part = jnp.stack(
        [
            jnp.stack(
                [
                    jnp.sum(
                        jnp.where((own_rows >= s * rows) & (own_rows < (s + 1) * rows), h * own_column, 0.0),
                        axis=(0, 2),
                    )
                    for s in range(subnets)
                ]
            )
            for h in own_history
        ]
    )
    far_fault = far_part
    for shift in range(1, nodes):
        far_fault = far_fault + lax.ppermute(
            far_part, "node", [(i, (i + shift) % nodes) for i in range(nodes)]
        )
    second = far_product(volts_all, column_all, all_info, currents, impedance)
    second = second.reshape(subnets, WINDOW_STEPS, cases, rows)

    results = []
    for instant in range(STEPS):
        turn = omega_step * instant
        open_volts = (
            math.cos(turn) * cos_volts
            - math.sin(turn) * sin_volts
            + base_volts[:, instant : instant + 1]
        )
        at_fault = source_fault(own_sums, instant)
        if instant >= WINDOW_STEPS:
            open_volts = open_volts + second[:, instant - WINDOW_STEPS]
            at_fault = at_fault + far_fault[instant - WINDOW_STEPS]
        current = jnp.where(fault_step <= instant, at_fault / denominator, 0.0)
        results.append(open_volts - current[:, :, None] * fault_column)
    return jnp.stack(results)


def solution(mesh):
    in_specs = (
        P("region", "node", None),
        P("region", None, "node"),
        P("region", "node"),
        P(None, ("region", "node")),
        P(None, ("region", "node")),
        P(("region", "node")),
        P(("region", "node")),
        P(("region", "node"), None),
        P("region", None),
        P("region", None),
        P("region", None),
    )
    out_specs = P(None, "region", None, "node")
    return jax.shard_map(
        functools.partial(body, mesh.shape["region"], mesh.shape["node"]),
        mesh=mesh,
        in_specs=in_specs,
        out_specs=out_specs,
        check_vma=False,
    )
```

```python
import functools
import math

import jax
import jax.numpy as jnp
from jax import lax
from jax.experimental import pallas as pl
from jax.experimental.pallas import tpu as pltpu
from jax.sharding import PartitionSpec as P

WINDOW_STEPS = 4
WINDOW_COUNT = 2
STEPS = WINDOW_STEPS * WINDOW_COUNT

omega_step = 2.0 * math.pi / 400.0
F32 = jnp.float32
BF16 = jnp.bfloat16


def base_kernel(taps_ref, incident_ref, base_ref, padded):
    tap_len = taps_ref.shape[0]
    past = incident_ref.shape[0]
    whole = past // 8 * 8
    padded[:whole, :] = incident_ref[:whole, :]
    padded[whole:, :] = jnp.zeros((padded.shape[0] - whole, padded.shape[1]), F32)
    padded[whole:past, :] = incident_ref[whole:past, :]

    def add_taps(block, total):
        start = pl.multiple_of(block * 8, 8)
        taps = taps_ref[pl.ds(start, 8), :]
        window = padded[pl.ds(pl.multiple_of(tap_len - 8 - start, 8), 16), :]
        for tap in range(8):
            total = total + taps[tap : tap + 1] * window[7 - tap : 15 - tap]
        return total

    base_ref[...] = lax.fori_loop(
        0, tap_len // 8, add_taps, jnp.zeros(base_ref.shape, F32), unroll=4
    )


def base_history(impulse_taps, incident):
    tap_len, ends = impulse_taps.shape
    past = incident.shape[0]
    columns = 512
    return pl.pallas_call(
        base_kernel,
        grid=(ends // columns,),
        in_specs=[
            pl.BlockSpec((tap_len, columns), lambda i: (0, i)),
            pl.BlockSpec((past, columns), lambda i: (0, i)),
        ],
        out_specs=pl.BlockSpec((STEPS, columns), lambda i: (0, i)),
        out_shape=jax.ShapeDtypeStruct((STEPS, ends), F32),
        scratch_shapes=[pltpu.VMEM(((tap_len + STEPS + 7) // 8 * 8, columns), F32)],
        compiler_params=pltpu.CompilerParams(vmem_limit_bytes=24 * 1024 * 1024),
    )(impulse_taps, incident)


def split(value):
    high = lax.reduce_precision(value, 8, 7)
    return high.astype(BF16), (value - high).astype(BF16)


def split_three(value):
    high = lax.reduce_precision(value, 8, 7)
    rest = value - high
    middle = lax.reduce_precision(rest, 8, 7)
    return high.astype(BF16), middle.astype(BF16), (rest - middle).astype(BF16)


def dot(a, b, dims):
    return lax.dot_general(a, b, dims, preferred_element_type=F32)


NT = (((1,), (1,)), ((), ()))


def exact_select(values, onehot):
    rows = values.shape[0]
    out = dot(jnp.concatenate(split_three(values), axis=0), onehot, (((1,), (0,)), ((), ())))
    return out[:rows] + out[rows : 2 * rows] + out[2 * rows :]


def select_rows(values, slot_map):
    rows = values.shape[0]
    out = dot(jnp.concatenate(split(values), axis=0), slot_map, NT)
    return out[:rows] + out[rows:]


def pieces(value):
    high = value.astype(BF16)
    return high, (value - high.astype(F32)).astype(BF16)


def block_product(x, z):
    count = x.shape[0]
    x_high, x_low = pieces(x)
    z_high, z_low = pieces(z)
    both = dot(jnp.concatenate([x_high, x_low], axis=0), z_high, NT)
    return both[:count] + both[count:] + dot(x_high, z_low, NT)


def accumulate(out_ref, index, first, value):
    @pl.when(first)
    def _():
        out_ref[index] = value

    @pl.when(jnp.logical_not(first))
    def _():
        out_ref[index] += value


def column_kernel(fault_ref, z_ref, out_ref):
    part = pl.program_id(1)
    cases = fault_ref.shape[1]
    depth = z_ref.shape[2]
    ids = lax.broadcasted_iota(jnp.int32, (cases, depth), 1) + part * depth
    onehot = jnp.where(fault_ref[0] == ids, 1.0, 0.0).astype(BF16)
    z_high, z_low = pieces(z_ref[0])
    value = dot(onehot, z_high, NT) + dot(onehot, z_low, NT)
    accumulate(out_ref, 0, part == 0, value)


def fault_columns(fault_node, impedance, parts):
    subnets, rows, order = impedance.shape
    cases = fault_node.shape[1]
    depth = order // parts
    return pl.pallas_call(
        column_kernel,
        grid=(subnets, parts),
        in_specs=[
            pl.BlockSpec((1, cases, 1), lambda s, n: (s, 0, 0)),
            pl.BlockSpec((1, rows, depth), lambda s, n: (s, 0, n)),
        ],
        out_specs=pl.BlockSpec((1, cases, rows), lambda s, n: (s, 0, 0)),
        out_shape=jax.ShapeDtypeStruct((subnets, cases, rows), F32),
        compiler_params=pltpu.CompilerParams(vmem_limit_bytes=52 * 1024 * 1024),
    )(fault_node[:, :, None], impedance)


def source_kernel(cases, x_ref, z_ref, out_ref):
    amp = x_ref[0, 0, :cases, :]
    hist = x_ref[0, 0, cases : cases + STEPS, :]
    angle = x_ref[0, 0, cases + STEPS : cases + STEPS + 1, :]
    x = jnp.concatenate([amp * jnp.cos(angle), amp * jnp.sin(angle), hist], axis=0)
    accumulate(out_ref, 0, pl.program_id(1) == 0, block_product(x, z_ref[0]))


def source_product(gathered, impedance, cases):
    parts, subnets, count, depth = gathered.shape
    rows = impedance.shape[1]
    total = 2 * cases + STEPS
    return pl.pallas_call(
        functools.partial(source_kernel, cases),
        grid=(subnets, parts),
        in_specs=[
            pl.BlockSpec((1, 1, count, depth), lambda s, n: (n, s, 0, 0)),
            pl.BlockSpec((1, rows, depth), lambda s, n: (s, 0, n)),
        ],
        out_specs=pl.BlockSpec((1, total, rows), lambda s, n: (s, 0, 0)),
        out_shape=jax.ShapeDtypeStruct((subnets, total, rows), F32),
        compiler_params=pltpu.CompilerParams(vmem_limit_bytes=52 * 1024 * 1024),
    )(gathered, impedance)


def far_waves(volts, column, currents):
    cases = currents[0][0].shape[-2]
    cos_wave = volts[..., :cases, :]
    sin_wave = volts[..., cases : 2 * cases, :]
    fault_wave = column[..., :cases, :]
    second_subnet = column[..., cases : cases + 1, :] > 0.5
    waves = []
    for instant in range(WINDOW_STEPS):
        turn = omega_step * instant
        free = volts[..., 2 * cases + instant : 2 * cases + instant + 1, :]
        current = jnp.where(second_subnet, currents[instant][1], currents[instant][0])
        waves.append(
            math.cos(turn) * cos_wave - math.sin(turn) * sin_wave + free - current * fault_wave
        )
    return waves


def far_history(waves, taps):
    history = []
    for offset in range(WINDOW_STEPS):
        total = taps[0] * waves[offset]
        for delay_index in range(1, offset + 1):
            total = total + taps[delay_index] * waves[offset - delay_index]
        history.append(total)
    return history


def far_kernel(volts_ref, column_ref, slot_ref, current_ref, z_ref, out_ref, high, low):
    first = pl.program_id(0) == 0
    sources = volts_ref.shape[0]
    lanes = volts_ref.shape[3]
    subnets, rows, depth = z_ref.shape
    flat = subnets * depth
    currents = [[current_ref[t, s] for s in range(subnets)] for t in range(WINDOW_STEPS)]
    slot_rows = []
    for source in range(sources):
        taps = [slot_ref[0, source, j : j + 1, :] for j in range(WINDOW_STEPS)]
        slot_rows.append(slot_ref[0, source, WINDOW_STEPS : WINDOW_STEPS + 1, :])
        waves = far_waves(volts_ref[source, 0], column_ref[source, 0], currents)
        history = jnp.concatenate(far_history(waves, taps), axis=0)
        one, two = pieces(history)
        high[:, source * lanes : (source + 1) * lanes] = one
        low[:, source * lanes : (source + 1) * lanes] = two
    slot_row = jnp.concatenate(slot_rows, axis=1).astype(jnp.int32)
    ids = lax.broadcasted_iota(jnp.int32, (flat, slot_row.shape[1]), 0)
    onehot = jnp.where(ids == slot_row, 1.0, 0.0).astype(BF16)
    injected = dot(high[...], onehot, NT) + dot(low[...], onehot, NT)
    for subnet in range(subnets):
        x = injected[:, subnet * depth : (subnet + 1) * depth]
        accumulate(out_ref, subnet, first, block_product(x, z_ref[subnet]))


def far_product(volts, column, slots, currents, impedance):
    sources, parts, volt_rows, lanes = volts.shape
    column_rows = column.shape[2]
    subnets, rows, order = impedance.shape
    cases = currents.shape[2]
    depth = order // parts
    total = WINDOW_STEPS * cases
    return pl.pallas_call(
        far_kernel,
        grid=(parts,),
        in_specs=[
            pl.BlockSpec((sources, 1, volt_rows, lanes), lambda n: (0, n, 0, 0)),
            pl.BlockSpec((sources, 1, column_rows, lanes), lambda n: (0, n, 0, 0)),
            pl.BlockSpec((1,) + slots.shape[1:], lambda n: (n, 0, 0, 0)),
            pl.BlockSpec(currents.shape, lambda n: (0, 0, 0, 0)),
            pl.BlockSpec((subnets, rows, depth), lambda n: (0, 0, n)),
        ],
        out_specs=pl.BlockSpec((subnets, total, rows), lambda n: (0, 0, 0)),
        out_shape=jax.ShapeDtypeStruct((subnets, total, rows), F32),
        scratch_shapes=[
            pltpu.VMEM((total, sources * lanes), BF16),
            pltpu.VMEM((total, sources * lanes), BF16),
        ],
        compiler_params=pltpu.CompilerParams(vmem_limit_bytes=52 * 1024 * 1024),
        cost_estimate=pl.CostEstimate(
            flops=6 * parts * total * rows * depth * subnets + 4 * parts * total * sources * lanes * subnets * depth,
            bytes_accessed=4 * (impedance.size + volts.size + column.size),
            transcendentals=0,
        ),
    )(volts, column, slots, currents, impedance)


def body(
    regions,
    nodes,
    impedance,
    source_amp,
    source_angle,
    impulse_taps,
    incident,
    conductance,
    attach,
    pair_slot,
    fault_node,
    fault_step,
    fault_res,
):
    subnets, rows, order = impedance.shape
    cases = source_amp.shape[1]
    ends = impulse_taps.shape[1]
    slots = ends // (regions * nodes)
    lanes = regions * slots
    flat = subnets * rows
    node = lax.axis_index("node")
    region = lax.axis_index("region")

    base = base_history(impulse_taps, incident)
    flat_ids = lax.iota(jnp.int32, flat)
    attach_map = (attach[:, None] == flat_ids[None, :]).astype(BF16)
    base_rows = exact_select(base, attach_map).reshape(STEPS, subnets, rows)
    payload = jnp.concatenate(
        [source_amp, jnp.transpose(base_rows, (1, 0, 2)), source_angle[:, None, :]], axis=1
    )
    gathered = lax.all_gather(payload, "node", axis=0, tiled=False)

    slot_row = pair_slot[0]
    end_ids = lax.iota(jnp.int32, ends)
    selector = end_ids[:, None] == slot_row[None, :]
    row_of_slot = jnp.sum(jnp.where(selector, attach[:, None] + 1, 0), axis=0) - 1
    slot_map = (row_of_slot[:, None] == flat_ids[None, :]).astype(BF16)
    end_values = jnp.concatenate(
        [2.0 * conductance[None, :], base[:WINDOW_STEPS], impulse_taps[:WINDOW_STEPS]], axis=0
    )
    slot_values = exact_select(end_values, selector.astype(BF16))
    slot_gain = slot_values[:1]
    slot_base = slot_values[1 : 1 + WINDOW_STEPS]
    slot_info = jnp.concatenate(
        [slot_values[1 + WINDOW_STEPS :], row_of_slot.astype(F32)[None, :]], axis=0
    )
    info_rows = slot_info.shape[0]
    own_info = jnp.transpose(
        slot_info.reshape(info_rows, regions, nodes, slots), (2, 0, 1, 3)
    ).reshape(nodes, info_rows, lanes)

    def to_region(block, more=None):
        count = block.shape[0]
        block = lax.all_to_all(block, "region", split_axis=1, concat_axis=1, tiled=True)
        block = block.reshape(count, regions, nodes, slots)
        block = jnp.transpose(block, (2, 0, 1, 3)).reshape(nodes, count, lanes)
        if more is not None:
            block = jnp.concatenate([block, more], axis=1)
        block = jnp.pad(block, ((0, 0), (0, -block.shape[1] % 8), (0, 0)))
        return block

    def by_flat(block):
        return jnp.transpose(block, (1, 0, 2)).reshape(block.shape[1], flat)

    fault_column = fault_columns(fault_node, impedance, nodes)
    column_slots = select_rows(by_flat(fault_column), slot_map)
    subnet_of_slot = (row_of_slot >= rows).astype(F32)[None, :]

    own_block = lax.dynamic_slice_in_dim(impedance, node * rows, rows, axis=2)
    row_ids = lax.iota(jnp.int32, rows)
    diagonal = jnp.sum(
        jnp.where((row_ids[:, None] == row_ids[None, :])[None], own_block, 0.0), axis=2
    )
    owner_mask = fault_node[:, :, None] == (node * rows + row_ids)[None, None, :]
    self_part = jnp.sum(jnp.where(owner_mask, diagonal[:, None, :], 0.0), axis=2)
    weighted = fault_column * source_amp
    cos_part = jnp.sum(weighted * jnp.cos(source_angle)[:, None, :], axis=2)
    sin_part = jnp.sum(weighted * jnp.sin(source_angle)[:, None, :], axis=2)
    base_part = jnp.einsum(
        "scr,tsr->tsc",
        fault_column,
        base_rows,
        precision=lax.Precision.HIGHEST,
        preferred_element_type=F32,
    )
    own_parts = jnp.concatenate(
        [
            jnp.stack([self_part, cos_part, sin_part]),
            base_part,
            jnp.stack([fault_res, fault_step.astype(F32)]),
        ],
        axis=0,
    )
    part_lanes = nodes * slots
    part_rows = -(-own_parts.size // part_lanes)
    part_block = jnp.pad(own_parts.reshape(-1), (0, part_rows * part_lanes - own_parts.size))
    part_block = jnp.broadcast_to(
        part_block.reshape(part_rows, 1, part_lanes), (part_rows, regions, part_lanes)
    ).reshape(part_rows, ends)
    column_count = cases + 1 + part_rows
    column_block = to_region(
        jnp.concatenate([slot_gain * column_slots, subnet_of_slot, part_block], axis=0), own_info
    )
    column_all = lax.all_gather(column_block, "node", axis=0, tiled=False)
    gathered, _ = lax.optimization_barrier((gathered, column_block))
    all_info = column_all[:, :, column_count : column_count + info_rows]
    all_parts = column_all[:, :, cases + 1 : column_count].reshape(
        nodes, nodes, part_rows, regions, slots
    )
    all_parts = jnp.transpose(all_parts, (3, 0, 2, 1, 4)).reshape(regions, nodes, -1)
    all_parts = all_parts[:, :, : own_parts.size].reshape((regions, nodes) + own_parts.shape)
    sums = jnp.sum(all_parts[:, :, : 3 + STEPS], axis=1)
    denominators = sums[:, 0] + all_parts[:, 0, 3 + STEPS]
    starts = all_parts[:, 0, 4 + STEPS]

    def source_fault(sums, instant):
        turn = omega_step * instant
        return (
            math.cos(turn) * sums[..., 1, :, :]
            - math.sin(turn) * sums[..., 2, :, :]
            + sums[..., 3 + instant, :, :]
        )

    currents = jnp.stack(
        [
            jnp.where(starts <= instant, source_fault(sums, instant) / denominators, 0.0)
            for instant in range(WINDOW_STEPS)
        ]
    )
    currents = jnp.transpose(currents, (0, 2, 3, 1))
    currents = jnp.broadcast_to(currents[..., None], currents.shape + (slots,))
    currents = currents.reshape(WINDOW_STEPS, subnets, cases, lanes)
    own_sums = lax.dynamic_index_in_dim(sums, region, axis=0, keepdims=False)
    denominator = own_sums[0] + fault_res

    first = source_product(gathered, impedance, cases)
    cos_volts = first[:, :cases]
    sin_volts = first[:, cases : 2 * cases]
    base_volts = first[:, 2 * cases :]
    volt_slots = slot_gain * select_rows(by_flat(first[:, : 2 * cases + WINDOW_STEPS]), slot_map)
    volts_block = to_region(
        jnp.concatenate([volt_slots[: 2 * cases], volt_slots[2 * cases :] - slot_base], axis=0)
    )
    volts_all = lax.all_gather(volts_block, "node", axis=0, tiled=False)

    info_own = jnp.transpose(own_info, (1, 0, 2))
    waves = far_waves(
        lax.dynamic_index_in_dim(volts_all, node, axis=1, keepdims=False),
        lax.dynamic_index_in_dim(column_all, node, axis=1, keepdims=False),
        [[currents[t, s][None] for s in range(subnets)] for t in range(WINDOW_STEPS)],
    )
    own_history = far_history(waves, [info_own[j][:, None, :] for j in range(WINDOW_STEPS)])
    own_column = jnp.transpose(
        column_slots.reshape(cases, regions, nodes, slots), (2, 0, 1, 3)
    ).reshape(nodes, cases, lanes)
    own_rows = info_own[WINDOW_STEPS][:, None, :]
    far_part = jnp.stack(
        [
            jnp.stack(
                [
                    jnp.sum(
                        jnp.where((own_rows >= s * rows) & (own_rows < (s + 1) * rows), h * own_column, 0.0),
                        axis=(0, 2),
                    )
                    for s in range(subnets)
                ]
            )
            for h in own_history
        ]
    )
    far_fault = far_part
    for shift in range(1, nodes):
        far_fault = far_fault + lax.ppermute(
            far_part, "node", [(i, (i + shift) % nodes) for i in range(nodes)]
        )
    second = far_product(volts_all, column_all, all_info, currents, impedance)
    second = second.reshape(subnets, WINDOW_STEPS, cases, rows)

    results = []
    for instant in range(STEPS):
        turn = omega_step * instant
        open_volts = (
            math.cos(turn) * cos_volts
            - math.sin(turn) * sin_volts
            + base_volts[:, instant : instant + 1]
        )
        at_fault = source_fault(own_sums, instant)
        if instant >= WINDOW_STEPS:
            open_volts = open_volts + second[:, instant - WINDOW_STEPS]
            at_fault = at_fault + far_fault[instant - WINDOW_STEPS]
        current = jnp.where(fault_step <= instant, at_fault / denominator, 0.0)
        results.append(open_volts - current[:, :, None] * fault_column)
    return jnp.stack(results)


def solution(mesh):
    in_specs = (
        P("region", "node", None),
        P("region", None, "node"),
        P("region", "node"),
        P(None, ("region", "node")),
        P(None, ("region", "node")),
        P(("region", "node")),
        P(("region", "node")),
        P(("region", "node"), None),
        P("region", None),
        P("region", None),
        P("region", None),
    )
    out_specs = P(None, "region", None, "node")
    return jax.shard_map(
        functools.partial(body, mesh.shape["region"], mesh.shape["node"]),
        mesh=mesh,
        in_specs=in_specs,
        out_specs=out_specs,
        check_vma=False,
    )
```
